32 devices in a mesh: grp: 4 (over y, core), sub: 8 (over z, x).
Axes of the slice: x: 2, y: 2, z: 4, core: 2. Of those that a mesh axis runs over, the one named last changes fastest.
Arguments:
- deflation: bfloat16 [32, 131072], P(None, ('grp', 'sub'))
- operator_blocks: bfloat16 [12288, 4096], P(('grp', 'sub'))
- diagonal: float32 [131072], P(('grp', 'sub'))
- block_rows: int32 [32, 384], P(('grp', 'sub')), may hold values from 0 to 63
- block_cols: int32 [32, 384], P(('grp', 'sub')), may hold values from 0 to 127, as said below
- live_count: int32 [32], P(('grp', 'sub')), may hold values from 96 to 384, as said below
- send_blocks: int32 [32, 4, 16], P(('grp', 'sub')), may hold values from 0 to 63
- residual: float32 [131072], P(('grp', 'sub')), may hold values from -6 to 6
Outputs:
- correction: float32 [131072], P(('grp', 'sub'))
- coarse_rows: float32 [32, 5120], P(('grp', 'sub'))
The draws below stay inside these ranges and needn't reach their ends.
Inputs may be any that keep to these rules, and one draw needn't show every extreme that they name: Slots from live_count on are padding and do not act; some subdomain uses all 384 slots and some uses exactly the least. `block_cols`: an even slot's column is below 64, the subdomain's own node block; an odd slot b's column lies in ghost region (b mod 8 + 1) / 2 - 1 of step one, numbered 0 to 3, each of 16 ghost blocks from 64 on. Several slots may share a position. `send_blocks`: A node block may be listed more than once.
All inputs are finite; a program needn't handle non-finite values.
Results may differ from the reference program's by a relative error of at most 0.00045.
Values may be sent and summed in bfloat16 or wider, within the bound.
A program may use at most 128 MiB of HBM per device.

```python
import math
import jax
import jax.numpy as jnp
from jax import lax

NV = 32
BS = 64
NODES = 64
BLK_PER = 6
SEND = 16
EXT = 128
BLK = 384
ROWS = 4096
N_GRP = 4
N_SUB = 8
DEVICES = 32


coupling_level = 4.2


def draw_deflation(key, part):
    key = jax.random.fold_in(key, 11)
    width = DEVICES * ROWS
    weights = jax.random.uniform(jax.random.fold_in(key, 1), (NV, 1), jnp.float32, 0.3, 0.7)
    profile = jax.random.uniform(jax.random.fold_in(key, 2), (1, width), jnp.float32, 0.5, 1.5)
    noise = jnp.clip(jax.random.normal(jax.random.fold_in(key, 3), (NV, width), jnp.float32), -4.0, 4.0)
    return (weights * profile + noise).astype(jnp.bfloat16)


def draw_operator_blocks(key, part):
    key = jax.random.fold_in(key, 23)
    spread = NODES ** 0.5 / 30.0
    offset_size = coupling_level * 8.0 / (BLK_PER * BS)
    slot_index = jnp.arange(DEVICES * BLK, dtype=jnp.int32) % BLK
    offset = jnp.where(slot_index % 2 == 1, -offset_size, 0.0).astype(jnp.float32)[:, None]
    noise = jnp.clip(jax.random.normal(key, (DEVICES * BLK, BS * BS), jnp.float32), -6.0, 6.0)
    return (spread * noise + offset).astype(jnp.bfloat16)


def draw_diagonal(key, part):
    key = jax.random.fold_in(key, 41)
    values = 4.0 * jnp.exp(jax.random.uniform(key, (DEVICES * ROWS,), jnp.float32, 0.0, math.log(4.0)))
    return values.astype(jnp.float32)


def draw_block_cols(key, part):
    key = jax.random.fold_in(key, 37)
    slot_index = jnp.arange(BLK, dtype=jnp.int32)[None, :]
    region = jnp.where(slot_index % 2 == 0, 0, (slot_index % 8 + 1) // 2)
    own_pick = jax.random.randint(jax.random.fold_in(key, 1), (DEVICES, BLK), 0, NODES)
    rim_pick = jax.random.randint(jax.random.fold_in(key, 2), (DEVICES, BLK), 0, SEND)
    return jnp.where(region == 0, own_pick, NODES + (region - 1) * SEND + rim_pick).astype(jnp.int32)


def draw_live_count(key, part):
    key = jax.random.fold_in(key, 53)
    least = max(BLK // 4, 1)
    counts = jax.random.randint(jax.random.fold_in(key, 1), (DEVICES,), least, BLK + 1)
    full_spot = jax.random.randint(jax.random.fold_in(key, 2), (), 0, DEVICES)
    light_spot = (full_spot + 1 + jax.random.randint(jax.random.fold_in(key, 3), (), 0, DEVICES - 1)) % DEVICES
    positions = jnp.arange(DEVICES)
    counts = jnp.where(positions == full_spot, BLK, counts)
    counts = jnp.where(positions == light_spot, least, counts)
    return counts.astype(jnp.int32)


def with_ends(entries, own_key, low, largest):
    dims = entries.shape
    index_at = [jax.random.randint(jax.random.fold_in(own_key, axis), (), 0, dims[axis]) for axis in range(len(dims))]
    entries = entries.at[tuple(index_at)].set(low)
    longest = dims.index(max(dims))
    index_at[longest] = (index_at[longest] + 1) % dims[longest]
    return entries.at[tuple(index_at)].set(largest)


def steps_of(rng, shape, split, low, high):
    def one(dim, parts):
        draws = jax.random.uniform(jax.random.fold_in(jax.random.fold_in(rng, 6), dim), (parts,), jnp.float32, low / len(split), high / len(split))
        return jnp.repeat(jnp.exp(draws), shape[dim] // parts).reshape((-1,) + (1,) * (len(shape) - dim - 1))

    level = one(*split[0])
    for cut in split[1:]:
        level = level * one(*cut)
    return level


def bell_draw(own_key, extent, scale, reach, split=(), kind=jnp.bfloat16):
    drawn = scale * jax.random.normal(own_key, extent, jnp.float32)
    if split:
        drawn = drawn * steps_of(own_key, extent, split, -0.22, 0.18)
    return jnp.clip(drawn, -reach, reach).astype(kind)


def setup_inputs(seed: int = 0) -> dict:
    streams_of = jax.random.split(jax.random.key(seed), 9)
    return {
        "deflation": draw_deflation(jax.random.fold_in(streams_of[8], 71), 0),
        "operator_blocks": draw_operator_blocks(jax.random.fold_in(streams_of[8], 71), 0),
        "diagonal": draw_diagonal(jax.random.fold_in(streams_of[8], 71), 0),
        "block_rows": with_ends(jax.random.randint(streams_of[3], (DEVICES, BLK), 0, NODES), jax.random.fold_in(streams_of[3], 1), 0, NODES - 1).astype(jnp.int32),
        "block_cols": draw_block_cols(jax.random.fold_in(streams_of[8], 71), 0),
        "live_count": draw_live_count(jax.random.fold_in(streams_of[8], 71), 0),
        "send_blocks": with_ends(jax.random.randint(streams_of[6], (DEVICES, 4, SEND), 0, NODES), jax.random.fold_in(streams_of[6], 1), 0, NODES - 1).astype(jnp.int32),
        "residual": bell_draw(streams_of[7], (DEVICES * ROWS,), 1.0, 6.0, ((0, 32),), jnp.float32),
    }


HIGHEST_PREC = lax.Precision.HIGHEST

def shift_tables(cycle_size):
    position = jnp.arange(cycle_size, dtype=jnp.int32)
    previous = (position - 1) % cycle_size
    following = (position + 1) % cycle_size
    same_block = position[:, None] == position[None, :]
    before_block = position[None, :] == previous[:, None]
    after_block = position[None, :] == following[:, None]
    return jnp.stack([same_block, before_block, after_block]).astype(jnp.float32)

def local_terms(device, deflation, operator_blocks, diagonal, block_rows, block_cols, live_count, send_blocks, residual):
    group_index = device // N_SUB
    sub_index = device % N_SUB
    sources = [group_index * N_SUB + (sub_index - 1) % N_SUB, group_index * N_SUB + (sub_index + 1) % N_SUB, (group_index - 1) * N_SUB + sub_index, (group_index + 1) * N_SUB + sub_index]
    present = [group_index >= 0, group_index >= 0, group_index > 0, group_index < N_GRP - 1]
    own_rows = lax.dynamic_slice_in_dim(deflation, (device * ROWS).astype(jnp.int32), ROWS, 1)
    regions = [own_rows]
    for region in range(4):
        source = jnp.clip(sources[region], 0, DEVICES - 1).astype(jnp.int32)
        node_tiles = lax.dynamic_slice_in_dim(deflation, (source * ROWS).astype(jnp.int32), ROWS, 1).reshape(NV, NODES, BS)
        chosen = send_blocks[source, region]
        piece = jnp.take(node_tiles, chosen, axis=1).reshape(NV, SEND * BS)
        regions.append(jnp.where(present[region], piece, jnp.zeros_like(piece)))
    extended = jnp.concatenate(regions, axis=1).reshape(NV, EXT, BS)
    col_ids = block_cols[device]
    row_ids = block_rows[device]
    picked = jnp.take(extended, col_ids, axis=1).astype(jnp.float32)
    block_mats = lax.dynamic_slice_in_dim(operator_blocks, (device * BLK).astype(jnp.int32), BLK, 0).reshape(BLK, BS, BS).astype(jnp.float32)
    products = jnp.einsum('bij,vbj->bvi', block_mats, picked, precision=HIGHEST_PREC)
    live_mask = (jnp.arange(BLK, dtype=jnp.int32) < live_count[device]).astype(jnp.float32)
    owners = jnp.where(col_ids < NODES, 0, 1 + (col_ids - NODES) // SEND)
    segment = (owners * NODES + row_ids).astype(jnp.int32)
    summed = jax.ops.segment_sum(products * live_mask[:, None, None], segment, num_segments=5 * NODES)
    applied = summed.reshape(5, NODES, NV, BS).transpose(0, 2, 1, 3).reshape(5, NV, ROWS)
    own_float = own_rows.astype(jnp.float32)
    own_diag = lax.dynamic_slice_in_dim(diagonal, (device * ROWS).astype(jnp.int32), ROWS, 0)
    applied = applied.at[0].add(own_diag[None, :] * own_float)
    coarse_rows = jnp.einsum('vr,owr->ovw', own_float, applied, precision=HIGHEST_PREC) / ROWS
    own_res = lax.dynamic_slice_in_dim(residual, (device * ROWS).astype(jnp.int32), ROWS, 0)
    coarse_rhs = jnp.dot(own_float, own_res, precision=HIGHEST_PREC) / 64.0
    return (coarse_rows, coarse_rhs)

def reference(deflation, operator_blocks, diagonal, block_rows, block_cols, live_count, send_blocks, residual):

    def one_device(device):
        return local_terms(device, deflation, operator_blocks, diagonal, block_rows, block_cols, live_count, send_blocks, residual)
    all_rows, all_rhs = lax.map(one_device, jnp.arange(DEVICES, dtype=jnp.int32))
    tables = shift_tables(N_SUB)
    group_rows = all_rows.reshape(N_GRP, N_SUB, 5, NV, NV)
    group_rhs = all_rhs.reshape(N_GRP, N_SUB * NV)

    def solve_group(operands):
        blocks, right_side = operands
        coarse_full = jnp.einsum('sovw,ost->svtw', blocks[:, :3], tables, precision=HIGHEST_PREC).reshape(N_SUB * NV, N_SUB * NV)
        symmetric = (coarse_full + coarse_full.T) * 0.5
        factor_low = jnp.linalg.cholesky(symmetric)
        return jax.scipy.linalg.cho_solve((factor_low, True), right_side)
    solved = lax.map(solve_group, (group_rows, group_rhs)).reshape(DEVICES, NV)
    vectors = deflation.astype(jnp.float32).reshape(NV, DEVICES, ROWS)
    correction = jnp.einsum('vdr,dv->dr', vectors, solved, precision=HIGHEST_PREC).reshape(DEVICES * ROWS)
    return (correction, all_rows.reshape(DEVICES, 5 * NV * NV))
```

```python
import functools

import jax
import jax.numpy as jnp
from jax import lax
from jax.experimental import pallas as pl
from jax.experimental.pallas import tpu as pltpu
from jax.sharding import PartitionSpec as P

NV = 32
BS = 64
NODES = 64
SEND = 16
BLK = 384
ROWS = 4096
LANES = 128
CHUNKS = ROWS // LANES
GROUP = 16
TURNS = BLK // GROUP
PARTS = 4

HIGHEST_PREC = lax.Precision.HIGHEST
MESH = pl.DeviceIdType.MESH
F32 = jnp.float32
BF16 = jnp.bfloat16


def dot_nt(a, b):
    return lax.dot_general(a, b, (((1,), (1,)), ((), ())), preferred_element_type=F32)


def hi_lo(values):
    upper = values.astype(BF16)
    lower = (values - upper.astype(F32)).astype(BF16)
    return jnp.concatenate([upper, lower], axis=0)


def assemble_kernel(
    n_grp, n_sub,
    rows_s, cols_s, live_s, send_s, z_ref, diag_ref, res_ref, a_hbm,
    strips, blocks,
    a_v, zs, zl, xn, out_b, ghost, wide, qs, strip, acc_own, acc_ghost,
    a_sem, ghost_send, ghost_recv, strip_send, strip_recv,
):
    grp = lax.axis_index("grp")
    sub = lax.axis_index("sub")
    following = lax.rem(sub + 1, n_sub)
    previous = lax.rem(sub + n_sub - 1, n_sub)
    has_lower = grp > 0
    has_upper = grp < n_grp - 1

    barrier = pltpu.get_barrier_semaphore()

    def greet(k, carry):
        pl.semaphore_signal(
            barrier, inc=1, device_id=(grp, lax.rem(sub + k, n_sub)), device_id_type=MESH
        )
        return carry

    lax.fori_loop(1, n_sub, greet, 0)

    @pl.when(has_lower)
    def _():
        pl.semaphore_signal(barrier, inc=1, device_id=(grp - 1, sub), device_id_type=MESH)

    @pl.when(has_upper)
    def _():
        pl.semaphore_signal(barrier, inc=1, device_id=(grp + 1, sub), device_id_type=MESH)

    part_rows = BLK // PARTS
    loads = [
        pltpu.make_async_copy(
            a_hbm.at[pl.ds(i * part_rows, part_rows)],
            a_v.at[pl.ds(i * part_rows, part_rows)],
            a_sem.at[i],
        )
        for i in range(PARTS)
    ]
    for load in loads:
        load.start()

    for c in range(CHUNKS):
        zs[c * NV:(c + 1) * NV, :] = z_ref[:, c * LANES:(c + 1) * LANES]
    source = lax.broadcasted_iota(jnp.int32, (LANES, LANES), 0)
    target = lax.broadcasted_iota(jnp.int32, (LANES, LANES), 1)
    for half in range(2):
        pick = (source == half * BS + lax.rem(target, BS)).astype(F32).astype(BF16)
        moved = jnp.dot(zs[...], pick, preferred_element_type=F32).astype(BF16)
        xn[:, half] = moved.reshape(CHUNKS, NV, LANES)
    for r in range(4):
        for c in range(SEND):
            node = send_s[0, r, c]
            out_b[r, c] = xn[lax.shift_right_logical(node, 1), lax.bitwise_and(node, 1)]

    pl.semaphore_wait(
        barrier, n_sub - 1 + has_lower.astype(jnp.int32) + has_upper.astype(jnp.int32)
    )

    def ghost_copy(r, device):
        return pltpu.make_async_remote_copy(
            src_ref=out_b.at[r], dst_ref=ghost.at[r], send_sem=ghost_send.at[r],
            recv_sem=ghost_recv.at[r], device_id=device, device_id_type=MESH,
        )

    to_next = ghost_copy(0, (grp, following))
    to_prev = ghost_copy(1, (grp, previous))
    to_upper = ghost_copy(2, (lax.rem(grp + 1, n_grp), sub))
    to_lower = ghost_copy(3, (lax.rem(grp + n_grp - 1, n_grp), sub))
    to_next.start()
    to_prev.start()

    @pl.when(has_upper)
    def _():
        to_upper.start()

    @pl.when(has_lower)
    def _():
        to_lower.start()

    @pl.when(jnp.logical_not(has_lower))
    def _():
        ghost[2] = jnp.zeros((SEND, NV, LANES), BF16)

    @pl.when(jnp.logical_not(has_upper))
    def _():
        ghost[3] = jnp.zeros((SEND, NV, LANES), BF16)

    for half in range(2):
        for parity in range(2):
            wanted = half * BS + 2 * target + parity
            pick = jnp.logical_and(source == wanted, target < BS // 2).astype(F32).astype(BF16)
            moved = jnp.dot(zs[...], pick, preferred_element_type=F32).astype(BF16)
            zl[:, half, parity * NV:(parity + 1) * NV] = moved.reshape(CHUNKS, NV, LANES)

    diag_sum = jnp.zeros((2 * NV, NV), F32)
    rhs_sum = jnp.zeros((NV, LANES), F32)
    for c in range(CHUNKS):
        z_c = z_ref[:, c * LANES:(c + 1) * LANES]
        z_f = z_c.astype(F32)
        diag_sum = diag_sum + dot_nt(hi_lo(z_f * diag_ref[c:c + 1, :]), z_c)
        rhs_sum = rhs_sum + z_f * res_ref[c:c + 1, :]
    rhs = jnp.sum(rhs_sum, axis=1, keepdims=True) * (1.0 / 64.0)

    low_half = lax.broadcasted_iota(jnp.int32, (NV, LANES), 1) < BS
    live = live_s[0]
    acc_own[...] = diag_sum
    acc_ghost[...] = jnp.zeros_like(acc_ghost)

    def turn_own(g, carry):
        base = pl.multiple_of(g * GROUP, GROUP)
        for m in range(BS // 2):
            slab = a_v[pl.ds(base, GROUP), m * LANES:(m + 1) * LANES].astype(F32)
            wide[pl.ds(m, GROUP, stride=BS // 2), :] = slab
        own_q = []
        own_x = []
        for t in range(GROUP):
            row = rows_s[0, base + t]
            left = zl[lax.shift_right_logical(row, 1), lax.bitwise_and(row, 1)][:, :BS // 2]
            block = wide[t * (BS // 2):(t + 1) * (BS // 2), :].astype(BF16)
            both = jnp.dot(left, block, preferred_element_type=F32)
            q = jnp.where(low_half, both[:NV], both[NV:])
            q = q * (base + t < live).astype(F32)
            q = hi_lo(q)
            if t % 2 == 0:
                col = cols_s[0, base + t]
                own_q.append(q)
                own_x.append(xn[lax.shift_right_logical(col, 1), lax.bitwise_and(col, 1)])
            else:
                qs[g, t // 2] = q
        acc_own[...] += dot_nt(
            jnp.concatenate(own_q, axis=1), jnp.concatenate(own_x, axis=1)
        )
        return carry

    turns = TURNS // PARTS
    for i in range(PARTS):
        loads[i].wait()
        lax.fori_loop(i * turns, (i + 1) * turns, turn_own, 0)

    to_next.wait()
    to_prev.wait()

    @pl.when(has_upper)
    def _():
        to_upper.wait_send()

    @pl.when(has_lower)
    def _():
        to_upper.wait_recv()

    @pl.when(has_lower)
    def _():
        to_lower.wait_send()

    @pl.when(has_upper)
    def _():
        to_lower.wait_recv()

    def turn_ghost(h, carry):
        for r in range(4):
            q_list = []
            x_list = []
            for e in range(2):
                g = 2 * h + e
                for t in (2 * r + 1, 2 * r + 9):
                    col = lax.bitwise_and(cols_s[0, g * GROUP + t], SEND - 1)
                    q_list.append(qs[g, t // 2])
                    x_list.append(ghost[r, col])
            acc_ghost[r] += dot_nt(
                jnp.concatenate(q_list, axis=1), jnp.concatenate(x_list, axis=1)
            )
        return carry

    lax.fori_loop(0, TURNS // 2, turn_ghost, 0)

    scale = 1.0 / ROWS
    coarse = [(acc_own[:NV] + acc_own[NV:]) * scale]
    for r in range(4):
        coarse.append((acc_ghost[r, :NV] + acc_ghost[r, NV:]) * scale)
    zero = jnp.zeros((NV, NV), F32)
    own, before, after = coarse[:3]
    flipped = jnp.transpose(jnp.concatenate([own, before, after, zero], axis=1))
    strip[:, :LANES] = jnp.concatenate(
        [
            (own + flipped[:NV]) * 0.5,
            before * 0.5,
            after * 0.5,
            jnp.broadcast_to(rhs, (NV, NV)),
        ],
        axis=1,
    )
    strip[:, LANES:] = jnp.concatenate(
        [zero, flipped[2 * NV:3 * NV] * 0.5, flipped[NV:2 * NV] * 0.5, zero], axis=1
    )

    def strip_copy(k, owner):
        return pltpu.make_async_remote_copy(
            src_ref=strip, dst_ref=strips.at[owner], send_sem=strip_send.at[k],
            recv_sem=strip_recv.at[owner], device_id=(grp, lax.rem(sub + k, n_sub)),
            device_id_type=MESH,
        )

    def send(k, carry):
        strip_copy(k, sub).start()
        return carry

    lax.fori_loop(1, n_sub, send, 0)
    strips[sub] = strip[...]
    for o in range(5):
        blocks[o * NV:(o + 1) * NV, :] = jnp.concatenate([coarse[o]] * 4, axis=1)

    def finish(k, carry):
        strip_copy(k, sub).wait_send()
        strip_copy(k, lax.rem(sub + n_sub - k, n_sub)).wait_recv()
        return carry

    lax.fori_loop(1, n_sub, finish, 0)


def eliminate(work):
    sub_row = lax.broadcasted_iota(jnp.int32, (1, NV, LANES), 1)
    for k in range(NV):
        row = work[:, k:k + 1, :]
        row = row * (1.0 / work[:, k:k + 1, k:k + 1])
        work = jnp.where(sub_row == k, row, work - work[:, :, k:k + 1] * row)
    return work


def dot_exact(a, b):
    return jnp.dot(a, b, precision=HIGHEST_PREC, preferred_element_type=F32)


def solve_blocks(systems):
    count = len(systems)
    if count == 1:
        return [eliminate(systems[0][None])[0][:, 3 * NV:]]
    odd = eliminate(jnp.stack(systems[1::2]))
    half = count // 2
    reduced = []
    zero = jnp.zeros((NV, NV), F32)
    for i in range(half):
        even = systems[2 * i]
        ahead, behind = odd[i], odd[(i - 1) % half]
        to_next, to_prev = even[:, 2 * NV:3 * NV], even[:, NV:2 * NV]
        if count == 2:
            gone = dot_exact(to_next + to_prev, ahead)
            link = gone[:, NV:2 * NV] + gone[:, 2 * NV:3 * NV]
            reduced.append(even - jnp.concatenate([link, zero, zero, gone[:, 3 * NV:]], axis=1))
            continue
        up = dot_exact(to_next, ahead)
        down = dot_exact(to_prev, behind)
        diag = even[:, :NV] - up[:, NV:2 * NV] - down[:, 2 * NV:3 * NV]
        right = even[:, 3 * NV:] - up[:, 3 * NV:] - down[:, 3 * NV:]
        reduced.append(
            jnp.concatenate([diag, -down[:, NV:2 * NV], -up[:, 2 * NV:3 * NV], right], axis=1)
        )
    evens = solve_blocks(reduced)
    solved = []
    for i in range(half):
        left, right = evens[i], evens[(i + 1) % half]
        gone = dot_exact(odd[i][:, NV:2 * NV], left) + dot_exact(odd[i][:, 2 * NV:3 * NV], right)
        solved += [left, odd[i][:, 3 * NV:] - gone]
    return solved


def solve_kernel(n_sub, strips, blocks, z_ref, corr, rows_out, found):
    systems = []
    lane = lax.broadcasted_iota(jnp.int32, (NV, LANES), 1)
    for s in range(n_sub):
        near = jnp.where(
            lane < 2 * NV, strips[(s - 1) % n_sub, :, LANES:], strips[(s + 1) % n_sub, :, LANES:]
        )
        systems.append(strips[s, :, :LANES] + near)
    solved = solve_blocks(systems)
    for s in range(n_sub):
        found[s] = jnp.concatenate([solved[s]] * 4, axis=1)
    own = found[lax.axis_index("sub")]
    for c in range(CHUNKS):
        z_c = z_ref[:, c * LANES:(c + 1) * LANES].astype(F32)
        corr[c:c + 1, :] = jnp.sum(z_c * own, axis=0, keepdims=True)
    lane8 = lax.broadcasted_iota(jnp.int32, (8, LANES), 1)
    for o in range(5):
        total = blocks[pl.ds(o * NV, 8, stride=4), :]
        for q in range(1, 4):
            total = jnp.where(
                lane8 >= q * NV, blocks[pl.ds(o * NV + q, 8, stride=4), :], total
            )
        rows_out[o * 8:(o + 1) * 8, :] = total


def per_device(
    n_grp, n_sub, deflation, operator_blocks, diagonal, block_rows, block_cols, live_count,
    send_blocks, residual,
):
    vmem = pl.BlockSpec(memory_space=pltpu.VMEM)
    smem = pl.BlockSpec(memory_space=pltpu.SMEM)
    strips, blocks = pl.pallas_call(
        functools.partial(assemble_kernel, n_grp, n_sub),
        out_shape=(
            jax.ShapeDtypeStruct((n_sub, NV, 2 * LANES), F32),
            jax.ShapeDtypeStruct((5 * NV, LANES), F32),
        ),
        in_specs=[smem] * 4 + [vmem] * 3 + [pl.BlockSpec(memory_space=pl.ANY)],
        out_specs=(vmem, vmem),
        scratch_shapes=[
            pltpu.VMEM((BLK, BS * BS), BF16),
            pltpu.VMEM((CHUNKS * NV, LANES), BF16),
            pltpu.VMEM((CHUNKS, 2, 2 * NV, LANES), BF16),
            pltpu.VMEM((CHUNKS, 2, NV, LANES), BF16),
            pltpu.VMEM((4, SEND, NV, LANES), BF16),
            pltpu.VMEM((4, SEND, NV, LANES), BF16),
            pltpu.VMEM((GROUP * BS // 2, LANES), F32),
            pltpu.VMEM((TURNS, GROUP // 2, 2 * NV, LANES), BF16),
            pltpu.VMEM((NV, 2 * LANES), F32),
            pltpu.VMEM((2 * NV, NV), F32),
            pltpu.VMEM((4, 2 * NV, NV), F32),
            pltpu.SemaphoreType.DMA((PARTS,)),
            pltpu.SemaphoreType.DMA((4,)),
            pltpu.SemaphoreType.DMA((4,)),
            pltpu.SemaphoreType.DMA((n_sub,)),
            pltpu.SemaphoreType.DMA((n_sub,)),
        ],
        compiler_params=pltpu.CompilerParams(
            collective_id=0, has_side_effects=True, vmem_limit_bytes=40 * 2**20
        ),
    )(
        block_rows, block_cols, live_count, send_blocks, deflation,
        diagonal.reshape(CHUNKS, LANES), residual.reshape(CHUNKS, LANES), operator_blocks,
    )
    correction, coarse_rows = pl.pallas_call(
        functools.partial(solve_kernel, n_sub),
        out_shape=(
            jax.ShapeDtypeStruct((CHUNKS, LANES), F32),
            jax.ShapeDtypeStruct((5 * NV * NV // LANES, LANES), F32),
        ),
        in_specs=[vmem] * 3,
        out_specs=(vmem, vmem),
        scratch_shapes=[pltpu.VMEM((n_sub, NV, LANES), F32)],
        compiler_params=pltpu.CompilerParams(vmem_limit_bytes=40 * 2**20),
    )(strips, blocks, deflation)
    return correction.reshape(ROWS), coarse_rows.reshape(1, 5 * NV * NV)


def solution(mesh):
    placed = (
        P(None, ("grp", "sub")),
        P(("grp", "sub"), None),
        P(("grp", "sub")),
        P(("grp", "sub"), None),
        P(("grp", "sub"), None),
        P(("grp", "sub")),
        P(("grp", "sub"), None, None),
        P(("grp", "sub")),
    )
    return jax.shard_map(
        functools.partial(per_device, mesh.shape["grp"], mesh.shape["sub"]),
        mesh=mesh,
        in_specs=placed,
        out_specs=(P(("grp", "sub")), P(("grp", "sub"), None)),
        check_vma=False,
    )
```

```python
import functools

import jax
import jax.numpy as jnp
from jax import lax
from jax.experimental import pallas as pl
from jax.experimental.pallas import tpu as pltpu
from jax.sharding import PartitionSpec as P

NV = 32
BS = 64
NODES = 64
SEND = 16
BLK = 384
ROWS = 4096
LANES = 128
CHUNKS = ROWS // LANES
GROUP = 16
TURNS = BLK // GROUP
PARTS = 4
PIVOTS = 4

HIGHEST_PREC = lax.Precision.HIGHEST
MESH = pl.DeviceIdType.MESH
F32 = jnp.float32
BF16 = jnp.bfloat16


def dot_nt(a, b):
    return lax.dot_general(a, b, (((1,), (1,)), ((), ())), preferred_element_type=F32)


def hi_lo(values):
    upper = values.astype(BF16)
    lower = (values - upper.astype(F32)).astype(BF16)
    return jnp.concatenate([upper, lower], axis=0)


def assemble_kernel(
    n_grp, n_sub,
    live_s, rows_h, cols_h, send_h, z_h, diag_h, res_h, a_hbm,
    strips, blocks,
    rows_s, cols_s, send_s, z_ref, diag_ref, res_ref, in_sem, a_v, zs, zl, xn, out_b, ghost, wide, qs, strip, acc_own, acc_ghost,
    a_sem, ghost_send, ghost_recv, strip_send, strip_recv,
):
    grp = lax.axis_index("grp")
    sub = lax.axis_index("sub")
    following = lax.rem(sub + 1, n_sub)
    previous = lax.rem(sub + n_sub - 1, n_sub)
    has_lower = grp > 0
    has_upper = grp < n_grp - 1

    pairs = [
        (z_h, z_ref), (send_h, send_s), (rows_h, rows_s), (cols_h, cols_s), (diag_h, diag_ref),
        (res_h, res_ref),
    ]
    inputs = [
        pltpu.make_async_copy(held, here, in_sem.at[i]) for i, (held, here) in enumerate(pairs)
    ]
    for copy in inputs:
        copy.start()
    barrier = pltpu.get_barrier_semaphore()

    def greet(k, carry):
        pl.semaphore_signal(
            barrier, inc=1, device_id=(grp, lax.rem(sub + k, n_sub)), device_id_type=MESH
        )
        return carry

    lax.fori_loop(1, n_sub, greet, 0)

    @pl.when(has_lower)
    def _():
        pl.semaphore_signal(barrier, inc=1, device_id=(grp - 1, sub), device_id_type=MESH)

    @pl.when(has_upper)
    def _():
        pl.semaphore_signal(barrier, inc=1, device_id=(grp + 1, sub), device_id_type=MESH)

    part_rows = BLK // PARTS
    loads = [
        pltpu.make_async_copy(
            a_hbm.at[pl.ds(i * part_rows, part_rows)],
            a_v.at[pl.ds(i * part_rows, part_rows)],
            a_sem.at[i],
        )
        for i in range(PARTS)
    ]
    for load in loads:
        load.start()

    inputs[0].wait()

    for c in range(CHUNKS):
        zs[c * NV:(c + 1) * NV, :] = z_ref[:, c * LANES:(c + 1) * LANES]
    source = lax.broadcasted_iota(jnp.int32, (LANES, LANES), 0)
    target = lax.broadcasted_iota(jnp.int32, (LANES, LANES), 1)
    for half in range(2):
        pick = (source == half * BS + lax.rem(target, BS)).astype(F32).astype(BF16)
        moved = jnp.dot(zs[...], pick, preferred_element_type=F32).astype(BF16)
        xn[:, half] = moved.reshape(CHUNKS, NV, LANES)
    inputs[1].wait()
    for r in range(4):
        for c in range(SEND):
            node = send_s[0, r, c]
            out_b[r, c] = xn[lax.shift_right_logical(node, 1), lax.bitwise_and(node, 1)]

    pl.semaphore_wait(
        barrier, n_sub - 1 + has_lower.astype(jnp.int32) + has_upper.astype(jnp.int32)
    )

    def ghost_copy(r, device):
        return pltpu.make_async_remote_copy(
            src_ref=out_b.at[r], dst_ref=ghost.at[r], send_sem=ghost_send.at[r],
            recv_sem=ghost_recv.at[r], device_id=device, device_id_type=MESH,
        )

    to_next = ghost_copy(0, (grp, following))
    to_prev = ghost_copy(1, (grp, previous))
    to_upper = ghost_copy(2, (lax.rem(grp + 1, n_grp), sub))
    to_lower = ghost_copy(3, (lax.rem(grp + n_grp - 1, n_grp), sub))
    to_next.start()
    to_prev.start()

    @pl.when(has_upper)
    def _():
        to_upper.start()

    @pl.when(has_lower)
    def _():
        to_lower.start()

    @pl.when(jnp.logical_not(has_lower))
    def _():
        ghost[2] = jnp.zeros((SEND, NV, LANES), BF16)

    @pl.when(jnp.logical_not(has_upper))
    def _():
        ghost[3] = jnp.zeros((SEND, NV, LANES), BF16)

    for half in range(2):
        for parity in range(2):
            wanted = half * BS + 2 * target + parity
            pick = jnp.logical_and(source == wanted, target < BS // 2).astype(F32).astype(BF16)
            moved = jnp.dot(zs[...], pick, preferred_element_type=F32).astype(BF16)
            zl[:, half, parity * NV:(parity + 1) * NV] = moved.reshape(CHUNKS, NV, LANES)

    for copy in inputs[2:]:
        copy.wait()

    diag_sum = jnp.zeros((2 * NV, NV), F32)
    rhs_sum = jnp.zeros((NV, LANES), F32)
    for c in range(CHUNKS):
        z_c = z_ref[:, c * LANES:(c + 1) * LANES]
        z_f = z_c.astype(F32)
        diag_sum = diag_sum + dot_nt(hi_lo(z_f * diag_ref[c:c + 1, :]), z_c)
        rhs_sum = rhs_sum + z_f * res_ref[c:c + 1, :]
    rhs = jnp.sum(rhs_sum, axis=1, keepdims=True) * (1.0 / 64.0)

    low_half = lax.broadcasted_iota(jnp.int32, (NV, LANES), 1) < BS
    live = live_s[0]
    acc_own[...] = diag_sum
    acc_ghost[...] = jnp.zeros_like(acc_ghost)

    def turn_own(g, carry):
        base = pl.multiple_of(g * GROUP, GROUP)
        for m in range(BS // 2):
            slab = a_v[pl.ds(base, GROUP), m * LANES:(m + 1) * LANES].astype(F32)
            wide[pl.ds(m, GROUP, stride=BS // 2), :] = slab
        own_q = []
        own_x = []
        for t in range(GROUP):
            row = rows_s[0, base + t]
            left = zl[lax.shift_right_logical(row, 1), lax.bitwise_and(row, 1)][:, :BS // 2]
            block = wide[t * (BS // 2):(t + 1) * (BS // 2), :].astype(BF16)
            both = jnp.dot(left, block, preferred_element_type=F32)
            q = jnp.where(low_half, both[:NV], both[NV:])
            q = q * (base + t < live).astype(F32)
            q = hi_lo(q)
            if t % 2 == 0:
                col = cols_s[0, base + t]
                own_q.append(q)
                own_x.append(xn[lax.shift_right_logical(col, 1), lax.bitwise_and(col, 1)])
            else:
                qs[g, t // 2] = q
        acc_own[...] += dot_nt(
            jnp.concatenate(own_q, axis=1), jnp.concatenate(own_x, axis=1)
        )
        return carry

    turns = TURNS // PARTS
    for i in range(PARTS):
        loads[i].wait()
        lax.fori_loop(i * turns, (i + 1) * turns, turn_own, 0)

    to_next.wait()
    to_prev.wait()

    @pl.when(has_upper)
    def _():
        to_upper.wait_send()

    @pl.when(has_lower)
    def _():
        to_upper.wait_recv()

    @pl.when(has_lower)
    def _():
        to_lower.wait_send()

    @pl.when(has_upper)
    def _():
        to_lower.wait_recv()

    def turn_ghost(h, carry):
        for r in range(4):
            q_list = []
            x_list = []
            for e in range(2):
                g = 2 * h + e
                for t in (2 * r + 1, 2 * r + 9):
                    col = lax.bitwise_and(cols_s[0, g * GROUP + t], SEND - 1)
                    q_list.append(qs[g, t // 2])
                    x_list.append(ghost[r, col])
            acc_ghost[r] += dot_nt(
                jnp.concatenate(q_list, axis=1), jnp.concatenate(x_list, axis=1)
            )
        return carry

    lax.fori_loop(0, TURNS // 2, turn_ghost, 0)

    scale = 1.0 / ROWS
    coarse = [(acc_own[:NV] + acc_own[NV:]) * scale]
    for r in range(4):
        coarse.append((acc_ghost[r, :NV] + acc_ghost[r, NV:]) * scale)
    zero = jnp.zeros((NV, NV), F32)
    own, before, after = coarse[:3]
    flipped = jnp.transpose(jnp.concatenate([own, before, after, zero], axis=1))
    strip[:, :LANES] = jnp.concatenate(
        [
            (own + flipped[:NV]) * 0.5,
            before * 0.5,
            after * 0.5,
            jnp.broadcast_to(rhs, (NV, NV)),
        ],
        axis=1,
    )
    strip[:, LANES:] = jnp.concatenate(
        [zero, flipped[2 * NV:3 * NV] * 0.5, flipped[NV:2 * NV] * 0.5, zero], axis=1
    )

    def strip_copy(k, owner):
        return pltpu.make_async_remote_copy(
            src_ref=strip, dst_ref=strips.at[owner], send_sem=strip_send.at[k],
            recv_sem=strip_recv.at[owner], device_id=(grp, lax.rem(sub + k, n_sub)),
            device_id_type=MESH,
        )

    def send(k, carry):
        strip_copy(k, sub).start()
        return carry

    lax.fori_loop(1, n_sub, send, 0)
    strips[sub] = strip[...]
    for o in range(5):
        blocks[o * NV:(o + 1) * NV, :] = jnp.concatenate([coarse[o]] * 4, axis=1)

    def finish(k, carry):
        strip_copy(k, sub).wait_send()
        strip_copy(k, lax.rem(sub + n_sub - k, n_sub)).wait_recv()
        return carry

    lax.fori_loop(1, n_sub, finish, 0)


def eliminate(work):
    row_of = lax.broadcasted_iota(jnp.int32, (1, NV, LANES), 1)
    for k in range(0, NV, PIVOTS):
        span = range(PIVOTS)
        cols = [jnp.broadcast_to(work[:, :, k + j:k + j + 1], work.shape) for j in span]
        small = [[cols[j][:, k + i:k + i + 1, :] for j in span] for i in span]
        rows = [work[:, k + i:k + i + 1, :] for i in span]
        for i in span:
            inverse = 1.0 / small[i][i]
            rows[i] = rows[i] * inverse
            for j in range(i + 1, PIVOTS):
                small[i][j] = small[i][j] * inverse
            for l in span:
                if l != i:
                    rows[l] = rows[l] - small[l][i] * rows[i]
                    for j in range(i + 1, PIVOTS):
                        small[l][j] = small[l][j] - small[l][i] * small[i][j]
        rest = work
        for j in span:
            rest = rest - cols[j] * rows[j]
        for i in span:
            rest = jnp.where(row_of == k + i, rows[i], rest)
        work = rest
    return work


def dot_exact(a, b):
    return jnp.dot(a, b, precision=HIGHEST_PREC, preferred_element_type=F32)


def solve_blocks(systems):
    count = len(systems)
    if count == 1:
        return [eliminate(systems[0][None])[0][:, 3 * NV:]]
    odd = eliminate(jnp.stack(systems[1::2]))
    half = count // 2
    reduced = []
    zero = jnp.zeros((NV, NV), F32)
    for i in range(half):
        even = systems[2 * i]
        ahead, behind = odd[i], odd[(i - 1) % half]
        to_next, to_prev = even[:, 2 * NV:3 * NV], even[:, NV:2 * NV]
        if count == 2:
            gone = dot_exact(to_next + to_prev, ahead)
            link = gone[:, NV:2 * NV] + gone[:, 2 * NV:3 * NV]
            reduced.append(even - jnp.concatenate([link, zero, zero, gone[:, 3 * NV:]], axis=1))
            continue
        up = dot_exact(to_next, ahead)
        down = dot_exact(to_prev, behind)
        diag = even[:, :NV] - up[:, NV:2 * NV] - down[:, 2 * NV:3 * NV]
        right = even[:, 3 * NV:] - up[:, 3 * NV:] - down[:, 3 * NV:]
        reduced.append(
            jnp.concatenate([diag, -down[:, NV:2 * NV], -up[:, 2 * NV:3 * NV], right], axis=1)
        )
    evens = solve_blocks(reduced)
    solved = []
    for i in range(half):
        left, right = evens[i], evens[(i + 1) % half]
        gone = dot_exact(odd[i][:, NV:2 * NV], left) + dot_exact(odd[i][:, 2 * NV:3 * NV], right)
        solved += [left, odd[i][:, 3 * NV:] - gone]
    return solved


def solve_kernel(n_sub, strips, blocks, z_ref, corr, rows_out, found):
    systems = []
    lane = lax.broadcasted_iota(jnp.int32, (NV, LANES), 1)
    for s in range(n_sub):
        near = jnp.where(
            lane < 2 * NV, strips[(s - 1) % n_sub, :, LANES:], strips[(s + 1) % n_sub, :, LANES:]
        )
        systems.append(strips[s, :, :LANES] + near)
    solved = solve_blocks(systems)
    for s in range(n_sub):
        found[s] = jnp.concatenate([solved[s]] * 4, axis=1)
    own = found[lax.axis_index("sub")]
    for c in range(CHUNKS):
        z_c = z_ref[:, c * LANES:(c + 1) * LANES].astype(F32)
        corr[c:c + 1, :] = jnp.sum(z_c * own, axis=0, keepdims=True)
    lane8 = lax.broadcasted_iota(jnp.int32, (8, LANES), 1)
    for o in range(5):
        total = blocks[pl.ds(o * NV, 8, stride=4), :]
        for q in range(1, 4):
            total = jnp.where(
                lane8 >= q * NV, blocks[pl.ds(o * NV + q, 8, stride=4), :], total
            )
        rows_out[o * 8:(o + 1) * 8, :] = total


def per_device(
    n_grp, n_sub, deflation, operator_blocks, diagonal, block_rows, block_cols, live_count,
    send_blocks, residual,
):
    vmem = pl.BlockSpec(memory_space=pltpu.VMEM)
    strips, blocks = pl.pallas_call(
        functools.partial(assemble_kernel, n_grp, n_sub),
        out_shape=(
            jax.ShapeDtypeStruct((n_sub, NV, 2 * LANES), F32),
            jax.ShapeDtypeStruct((5 * NV, LANES), F32),
        ),
        in_specs=[pl.BlockSpec(memory_space=pltpu.SMEM)]
        + [pl.BlockSpec(memory_space=pltpu.HBM)] * 7,
        out_specs=(vmem, vmem),
        scratch_shapes=[
            pltpu.SMEM((1, BLK), jnp.int32),
            pltpu.SMEM((1, BLK), jnp.int32),
            pltpu.SMEM((1, 4, SEND), jnp.int32),
            pltpu.VMEM((NV, ROWS), BF16),
            pltpu.VMEM((CHUNKS, LANES), F32),
            pltpu.VMEM((CHUNKS, LANES), F32),
            pltpu.SemaphoreType.DMA((6,)),
            pltpu.VMEM((BLK, BS * BS), BF16),
            pltpu.VMEM((CHUNKS * NV, LANES), BF16),
            pltpu.VMEM((CHUNKS, 2, 2 * NV, LANES), BF16),
            pltpu.VMEM((CHUNKS, 2, NV, LANES), BF16),
            pltpu.VMEM((4, SEND, NV, LANES), BF16),
            pltpu.VMEM((4, SEND, NV, LANES), BF16),
            pltpu.VMEM((GROUP * BS // 2, LANES), F32),
            pltpu.VMEM((TURNS, GROUP // 2, 2 * NV, LANES), BF16),
            pltpu.VMEM((NV, 2 * LANES), F32),
            pltpu.VMEM((2 * NV, NV), F32),
            pltpu.VMEM((4, 2 * NV, NV), F32),
            pltpu.SemaphoreType.DMA((PARTS,)),
            pltpu.SemaphoreType.DMA((4,)),
            pltpu.SemaphoreType.DMA((4,)),
            pltpu.SemaphoreType.DMA((n_sub,)),
            pltpu.SemaphoreType.DMA((n_sub,)),
        ],
        compiler_params=pltpu.CompilerParams(
            collective_id=0, has_side_effects=True, vmem_limit_bytes=40 * 2**20
        ),
    )(
        live_count,
        *[
            pltpu.with_memory_space_constraint(held, pltpu.HBM)
            for held in (
                block_rows, block_cols, send_blocks, deflation,
                diagonal.reshape(CHUNKS, LANES), residual.reshape(CHUNKS, LANES), operator_blocks,
            )
        ],
    )
    correction, coarse_rows = pl.pallas_call(
        functools.partial(solve_kernel, n_sub),
        out_shape=(
            jax.ShapeDtypeStruct((CHUNKS, LANES), F32),
            jax.ShapeDtypeStruct((5 * NV * NV // LANES, LANES), F32),
        ),
        in_specs=[vmem] * 3,
        out_specs=(vmem, vmem),
        scratch_shapes=[pltpu.VMEM((n_sub, NV, LANES), F32)],
        compiler_params=pltpu.CompilerParams(vmem_limit_bytes=40 * 2**20),
    )(strips, blocks, deflation)
    return correction.reshape(ROWS), coarse_rows.reshape(1, 5 * NV * NV)


def solution(mesh):
    placed = (
        P(None, ("grp", "sub")),
        P(("grp", "sub"), None),
        P(("grp", "sub")),
        P(("grp", "sub"), None),
        P(("grp", "sub"), None),
        P(("grp", "sub")),
        P(("grp", "sub"), None, None),
        P(("grp", "sub")),
    )
    return jax.shard_map(
        functools.partial(per_device, mesh.shape["grp"], mesh.shape["sub"]),
        mesh=mesh,
        in_specs=placed,
        out_specs=(P(("grp", "sub")), P(("grp", "sub"), None)),
        check_vma=False,
    )
```

```python
import functools

import jax
import jax.numpy as jnp
from jax import lax
from jax.experimental import pallas as pl
from jax.experimental.pallas import tpu as pltpu
from jax.sharding import PartitionSpec as P

NV = 32
BS = 64
NODES = 64
SEND = 16
BLK = 384
ROWS = 4096
LANES = 128
CHUNKS = ROWS // LANES
GROUP = 16
TURNS = BLK // GROUP
PARTS = 4
PIVOTS = 4
PITCH = 40

HIGHEST_PREC = lax.Precision.HIGHEST
MESH = pl.DeviceIdType.MESH
F32 = jnp.float32
BF16 = jnp.bfloat16


def dot_nt(a, b):
    return lax.dot_general(a, b, (((1,), (1,)), ((), ())), preferred_element_type=F32)


def hi_lo(values):
    upper = values.astype(BF16)
    lower = (values - upper.astype(F32)).astype(BF16)
    return jnp.concatenate([upper, lower], axis=0)


def assemble_kernel(
    n_grp, n_sub,
    live_s, rows_h, cols_h, send_h, z_h, diag_h, res_h, a_hbm,
    strips, blocks,
    rows_s, cols_s, send_s, z_ref, diag_ref, res_ref, in_sem, a_v, zs, zl, xn, out_b, ghost, wide, qs, strip, acc_own, acc_ghost,
    a_sem, ghost_send, ghost_recv, strip_send, strip_recv,
):
    grp = lax.axis_index("grp")
    sub = lax.axis_index("sub")
    following = lax.rem(sub + 1, n_sub)
    previous = lax.rem(sub + n_sub - 1, n_sub)
    has_lower = grp > 0
    has_upper = grp < n_grp - 1

    pairs = [
        (z_h, z_ref), (send_h, send_s), (rows_h, rows_s), (cols_h, cols_s), (diag_h, diag_ref),
        (res_h, res_ref),
    ]
    inputs = [
        pltpu.make_async_copy(held, here, in_sem.at[i]) for i, (held, here) in enumerate(pairs)
    ]
    for copy in inputs:
        copy.start()
    barrier = pltpu.get_barrier_semaphore()

    def greet(k, carry):
        pl.semaphore_signal(
            barrier, inc=1, device_id=(grp, lax.rem(sub + k, n_sub)), device_id_type=MESH
        )
        return carry

    lax.fori_loop(1, n_sub, greet, 0)

    @pl.when(has_lower)
    def _():
        pl.semaphore_signal(barrier, inc=1, device_id=(grp - 1, sub), device_id_type=MESH)

    @pl.when(has_upper)
    def _():
        pl.semaphore_signal(barrier, inc=1, device_id=(grp + 1, sub), device_id_type=MESH)

    part_rows = BLK // PARTS
    loads = [
        pltpu.make_async_copy(
            a_hbm.at[pl.ds(i * part_rows, part_rows)],
            a_v.at[pl.ds(i * part_rows, part_rows)],
            a_sem.at[i],
        )
        for i in range(PARTS)
    ]
    for load in loads:
        load.start()

    inputs[0].wait()

    for c in range(CHUNKS):
        zs[c * NV:(c + 1) * NV, :] = z_ref[:, c * LANES:(c + 1) * LANES]
    source = lax.broadcasted_iota(jnp.int32, (LANES, LANES), 0)
    target = lax.broadcasted_iota(jnp.int32, (LANES, LANES), 1)
    for half in range(2):
        pick = (source == half * BS + lax.rem(target, BS)).astype(F32).astype(BF16)
        moved = jnp.dot(zs[...], pick, preferred_element_type=F32).astype(BF16)
        xn[:, half] = moved.reshape(CHUNKS, NV, LANES)
    inputs[1].wait()
    for r in range(4):
        for c in range(SEND):
            node = send_s[0, r, c]
            out_b[r, c] = xn[lax.shift_right_logical(node, 1), lax.bitwise_and(node, 1)]

    pl.semaphore_wait(
        barrier, n_sub - 1 + has_lower.astype(jnp.int32) + has_upper.astype(jnp.int32)
    )

    def ghost_copy(r, device):
        return pltpu.make_async_remote_copy(
            src_ref=out_b.at[r], dst_ref=ghost.at[r], send_sem=ghost_send.at[r],
            recv_sem=ghost_recv.at[r], device_id=device, device_id_type=MESH,
        )

    to_next = ghost_copy(0, (grp, following))
    to_prev = ghost_copy(1, (grp, previous))
    to_upper = ghost_copy(2, (lax.rem(grp + 1, n_grp), sub))
    to_lower = ghost_copy(3, (lax.rem(grp + n_grp - 1, n_grp), sub))
    to_next.start()
    to_prev.start()

    @pl.when(has_upper)
    def _():
        to_upper.start()

    @pl.when(has_lower)
    def _():
        to_lower.start()

    @pl.when(jnp.logical_not(has_lower))
    def _():
        ghost[2] = jnp.zeros((SEND, NV, LANES), BF16)

    @pl.when(jnp.logical_not(has_upper))
    def _():
        ghost[3] = jnp.zeros((SEND, NV, LANES), BF16)

    for half in range(2):
        for parity in range(2):
            wanted = half * BS + 2 * target + parity
            pick = jnp.logical_and(source == wanted, target < BS // 2).astype(F32).astype(BF16)
            moved = jnp.dot(zs[...], pick, preferred_element_type=F32).astype(BF16)
            zl[:, half, parity * NV:(parity + 1) * NV] = moved.reshape(CHUNKS, NV, LANES)

    for copy in inputs[2:]:
        copy.wait()

    diag_sum = jnp.zeros((2 * NV, NV), F32)
    rhs_sum = jnp.zeros((NV, LANES), F32)
    for c in range(CHUNKS):
        z_c = z_ref[:, c * LANES:(c + 1) * LANES]
        z_f = z_c.astype(F32)
        diag_sum = diag_sum + dot_nt(hi_lo(z_f * diag_ref[c:c + 1, :]), z_c)
        rhs_sum = rhs_sum + z_f * res_ref[c:c + 1, :]
    rhs = jnp.sum(rhs_sum, axis=1, keepdims=True) * (1.0 / 64.0)

    low_half = lax.broadcasted_iota(jnp.int32, (NV, LANES), 1) < BS
    live = live_s[0]
    acc_own[...] = diag_sum
    acc_ghost[...] = jnp.zeros_like(acc_ghost)

    def turn_own(g, carry):
        base = pl.multiple_of(g * GROUP, GROUP)
        for m in range(BS // 2):
            slab = a_v[pl.ds(base, GROUP), m * LANES:(m + 1) * LANES].astype(F32)
            wide[pl.ds(m, GROUP, stride=PITCH), :] = slab
        own_q = []
        own_x = []
        for t in range(GROUP):
            row = rows_s[0, base + t]
            left = zl[lax.shift_right_logical(row, 1), lax.bitwise_and(row, 1)][:, :BS // 2]
            block = wide[t * PITCH:t * PITCH + BS // 2, :].astype(BF16)
            both = jnp.dot(left, block, preferred_element_type=F32)
            q = jnp.where(low_half, both[:NV], both[NV:])
            q = q * (base + t < live).astype(F32)
            q = hi_lo(q)
            if t % 2 == 0:
                col = cols_s[0, base + t]
                own_q.append(q)
                own_x.append(xn[lax.shift_right_logical(col, 1), lax.bitwise_and(col, 1)])
            else:
                qs[g, t // 2] = q
        acc_own[...] += dot_nt(
            jnp.concatenate(own_q, axis=1), jnp.concatenate(own_x, axis=1)
        )
        return carry

    turns = TURNS // PARTS
    for i in range(PARTS):
        loads[i].wait()
        lax.fori_loop(i * turns, (i + 1) * turns, turn_own, 0)

    to_next.wait()
    to_prev.wait()

    @pl.when(has_upper)
    def _():
        to_upper.wait_send()

    @pl.when(has_lower)
    def _():
        to_upper.wait_recv()

    @pl.when(has_lower)
    def _():
        to_lower.wait_send()

    @pl.when(has_upper)
    def _():
        to_lower.wait_recv()

    def turn_ghost(h, carry):
        for r in range(4):
            q_list = []
            x_list = []
            for e in range(2):
                g = 2 * h + e
                for t in (2 * r + 1, 2 * r + 9):
                    col = lax.bitwise_and(cols_s[0, g * GROUP + t], SEND - 1)
                    q_list.append(qs[g, t // 2])
                    x_list.append(ghost[r, col])
            acc_ghost[r] += dot_nt(
                jnp.concatenate(q_list, axis=1), jnp.concatenate(x_list, axis=1)
            )
        return carry

    lax.fori_loop(0, TURNS // 2, turn_ghost, 0)

    scale = 1.0 / ROWS
    coarse = [(acc_own[:NV] + acc_own[NV:]) * scale]
    for r in range(4):
        coarse.append((acc_ghost[r, :NV] + acc_ghost[r, NV:]) * scale)
    own, before, after = coarse[:3]
    strip[...] = jnp.concatenate(
        [
            (own + jnp.transpose(own)) * 0.5,
            before * 0.5,
            after * 0.5,
            jnp.broadcast_to(rhs, (NV, NV)),
        ],
        axis=1,
    )

    def strip_copy(k, owner):
        return pltpu.make_async_remote_copy(
            src_ref=strip, dst_ref=strips.at[owner], send_sem=strip_send.at[k],
            recv_sem=strip_recv.at[owner], device_id=(grp, lax.rem(sub + k, n_sub)),
            device_id_type=MESH,
        )

    def send(k, carry):
        strip_copy(k, sub).start()
        return carry

    lax.fori_loop(1, n_sub, send, 0)
    strips[sub] = strip[...]
    for o in range(5):
        blocks[o * NV:(o + 1) * NV, :] = jnp.concatenate([coarse[o]] * 4, axis=1)

    def finish(k, carry):
        strip_copy(k, sub).wait_send()
        strip_copy(k, lax.rem(sub + n_sub - k, n_sub)).wait_recv()
        return carry

    lax.fori_loop(1, n_sub, finish, 0)


def eliminate(work):
    row_of = lax.broadcasted_iota(jnp.int32, (1, NV, LANES), 1)
    for k in range(0, NV, PIVOTS):
        span = range(PIVOTS)
        cols = [jnp.broadcast_to(work[:, :, k + j:k + j + 1], work.shape) for j in span]
        small = [[cols[j][:, k + i:k + i + 1, :] for j in span] for i in span]
        rows = [work[:, k + i:k + i + 1, :] for i in span]
        for i in span:
            inverse = 1.0 / small[i][i]
            rows[i] = rows[i] * inverse
            for j in range(i + 1, PIVOTS):
                small[i][j] = small[i][j] * inverse
            for l in span:
                if l != i:
                    rows[l] = rows[l] - small[l][i] * rows[i]
                    for j in range(i + 1, PIVOTS):
                        small[l][j] = small[l][j] - small[l][i] * small[i][j]
        rest = work
        for j in span:
            rest = rest - cols[j] * rows[j]
        for i in span:
            rest = jnp.where(row_of == k + i, rows[i], rest)
        work = rest
    return work


def dot_exact(a, b):
    return jnp.dot(a, b, precision=HIGHEST_PREC, preferred_element_type=F32)


def solve_blocks(systems):
    count = len(systems)
    if count == 1:
        return [eliminate(systems[0][None])[0][:, 3 * NV:]]
    odd = eliminate(jnp.stack(systems[1::2]))
    half = count // 2
    reduced = []
    zero = jnp.zeros((NV, NV), F32)
    for i in range(half):
        even = systems[2 * i]
        ahead, behind = odd[i], odd[(i - 1) % half]
        to_next, to_prev = even[:, 2 * NV:3 * NV], even[:, NV:2 * NV]
        if count == 2:
            gone = dot_exact(to_next + to_prev, ahead)
            link = gone[:, NV:2 * NV] + gone[:, 2 * NV:3 * NV]
            reduced.append(even - jnp.concatenate([link, zero, zero, gone[:, 3 * NV:]], axis=1))
            continue
        up = dot_exact(to_next, ahead)
        down = dot_exact(to_prev, behind)
        diag = even[:, :NV] - up[:, NV:2 * NV] - down[:, 2 * NV:3 * NV]
        right = even[:, 3 * NV:] - up[:, 3 * NV:] - down[:, 3 * NV:]
        reduced.append(
            jnp.concatenate([diag, -down[:, NV:2 * NV], -up[:, 2 * NV:3 * NV], right], axis=1)
        )
    evens = solve_blocks(reduced)
    solved = []
    for i in range(half):
        left, right = evens[i], evens[(i + 1) % half]
        gone = dot_exact(odd[i][:, NV:2 * NV], left) + dot_exact(odd[i][:, 2 * NV:3 * NV], right)
        solved += [left, odd[i][:, 3 * NV:] - gone]
    return solved


def solve_kernel(n_sub, strips, blocks, z_ref, corr, rows_out, found):
    systems = []
    zero = jnp.zeros((NV, NV), F32)
    flipped = [jnp.transpose(strips[s]) for s in range(n_sub)]
    for s in range(n_sub):
        from_prev = flipped[(s - 1) % n_sub][2 * NV:3 * NV]
        from_next = flipped[(s + 1) % n_sub][NV:2 * NV]
        systems.append(strips[s] + jnp.concatenate([zero, from_prev, from_next, zero], axis=1))
    solved = solve_blocks(systems)
    for s in range(n_sub):
        found[s] = jnp.concatenate([solved[s]] * 4, axis=1)
    own = found[lax.axis_index("sub")]
    for c in range(CHUNKS):
        z_c = z_ref[:, c * LANES:(c + 1) * LANES].astype(F32)
        corr[c:c + 1, :] = jnp.sum(z_c * own, axis=0, keepdims=True)
    lane8 = lax.broadcasted_iota(jnp.int32, (8, LANES), 1)
    for o in range(5):
        total = blocks[pl.ds(o * NV, 8, stride=4), :]
        for q in range(1, 4):
            total = jnp.where(
                lane8 >= q * NV, blocks[pl.ds(o * NV + q, 8, stride=4), :], total
            )
        rows_out[o * 8:(o + 1) * 8, :] = total


def per_device(
    n_grp, n_sub, deflation, operator_blocks, diagonal, block_rows, block_cols, live_count,
    send_blocks, residual,
):
    vmem = pl.BlockSpec(memory_space=pltpu.VMEM)
    strips, blocks = pl.pallas_call(
        functools.partial(assemble_kernel, n_grp, n_sub),
        out_shape=(
            jax.ShapeDtypeStruct((n_sub, NV, LANES), F32),
            jax.ShapeDtypeStruct((5 * NV, LANES), F32),
        ),
        in_specs=[pl.BlockSpec(memory_space=pltpu.SMEM)]
        + [pl.BlockSpec(memory_space=pltpu.HBM)] * 7,
        out_specs=(vmem, vmem),
        scratch_shapes=[
            pltpu.SMEM((1, BLK), jnp.int32),
            pltpu.SMEM((1, BLK), jnp.int32),
            pltpu.SMEM((1, 4, SEND), jnp.int32),
            pltpu.VMEM((NV, ROWS), BF16),
            pltpu.VMEM((CHUNKS, LANES), F32),
            pltpu.VMEM((CHUNKS, LANES), F32),
            pltpu.SemaphoreType.DMA((6,)),
            pltpu.VMEM((BLK, BS * BS), BF16),
            pltpu.VMEM((CHUNKS * NV, LANES), BF16),
            pltpu.VMEM((CHUNKS, 2, 2 * NV, LANES), BF16),
            pltpu.VMEM((CHUNKS, 2, NV, LANES), BF16),
            pltpu.VMEM((4, SEND, NV, LANES), BF16),
            pltpu.VMEM((4, SEND, NV, LANES), BF16),
            pltpu.VMEM((GROUP * PITCH, LANES), F32),
            pltpu.VMEM((TURNS, GROUP // 2, 2 * NV, LANES), BF16),
            pltpu.VMEM((NV, LANES), F32),
            pltpu.VMEM((2 * NV, NV), F32),
            pltpu.VMEM((4, 2 * NV, NV), F32),
            pltpu.SemaphoreType.DMA((PARTS,)),
            pltpu.SemaphoreType.DMA((4,)),
            pltpu.SemaphoreType.DMA((4,)),
            pltpu.SemaphoreType.DMA((n_sub,)),
            pltpu.SemaphoreType.DMA((n_sub,)),
        ],
        compiler_params=pltpu.CompilerParams(
            collective_id=0, has_side_effects=True, vmem_limit_bytes=40 * 2**20
        ),
    )(
        live_count,
        *[
            pltpu.with_memory_space_constraint(held, pltpu.HBM)
            for held in (
                block_rows, block_cols, send_blocks, deflation,
                diagonal.reshape(CHUNKS, LANES), residual.reshape(CHUNKS, LANES), operator_blocks,
            )
        ],
    )
    correction, coarse_rows = pl.pallas_call(
        functools.partial(solve_kernel, n_sub),
        out_shape=(
            jax.ShapeDtypeStruct((CHUNKS, LANES), F32),
            jax.ShapeDtypeStruct((5 * NV * NV // LANES, LANES), F32),
        ),
        in_specs=[vmem] * 3,
        out_specs=(vmem, vmem),
        scratch_shapes=[pltpu.VMEM((n_sub, NV, LANES), F32)],
        compiler_params=pltpu.CompilerParams(vmem_limit_bytes=40 * 2**20),
    )(strips, blocks, deflation)
    return correction.reshape(ROWS), coarse_rows.reshape(1, 5 * NV * NV)


def solution(mesh):
    placed = (
        P(None, ("grp", "sub")),
        P(("grp", "sub"), None),
        P(("grp", "sub")),
        P(("grp", "sub"), None),
        P(("grp", "sub"), None),
        P(("grp", "sub")),
        P(("grp", "sub"), None, None),
        P(("grp", "sub")),
    )
    return jax.shard_map(
        functools.partial(per_device, mesh.shape["grp"], mesh.shape["sub"]),
        mesh=mesh,
        in_specs=placed,
        out_specs=(P(("grp", "sub")), P(("grp", "sub"), None)),
        check_vma=False,
    )
```

```python
import functools

import jax
import jax.numpy as jnp
from jax import lax
from jax.experimental import pallas as pl
from jax.experimental.pallas import tpu as pltpu
from jax.sharding import PartitionSpec as P

NV = 32
BS = 64
NODES = 64
SEND = 16
BLK = 384
ROWS = 4096
LANES = 128
CHUNKS = ROWS // LANES
GROUP = 16
TURNS = BLK // GROUP
PARTS = 4
PIVOTS = 4
PITCH = 40

HIGHEST_PREC = lax.Precision.HIGHEST
MESH = pl.DeviceIdType.MESH
F32 = jnp.float32
BF16 = jnp.bfloat16


def dot_nt(a, b):
    return lax.dot_general(a, b, (((1,), (1,)), ((), ())), preferred_element_type=F32)


def hi_lo(values):
    upper = values.astype(BF16)
    lower = (values - upper.astype(F32)).astype(BF16)
    return jnp.concatenate([upper, lower], axis=0)


def assemble_kernel(
    n_grp, n_sub,
    live_s, rows_h, cols_h, send_h, z_h, diag_h, res_h, a_hbm,
    strips, blocks,
    rows_s, cols_s, send_s, z_ref, diag_ref, res_ref, in_sem, a_v, zs, zl, xn, out_b, ghost, wide, qs, strip, acc_own, acc_ghost,
    a_sem, ghost_send, ghost_recv, strip_send, strip_recv,
):
    grp = lax.axis_index("grp")
    sub = lax.axis_index("sub")
    following = lax.rem(sub + 1, n_sub)
    previous = lax.rem(sub + n_sub - 1, n_sub)
    has_lower = grp > 0
    has_upper = grp < n_grp - 1

    pairs = [
        (z_h, z_ref), (send_h, send_s), (rows_h, rows_s), (cols_h, cols_s), (diag_h, diag_ref),
        (res_h, res_ref),
    ]
    inputs = [
        pltpu.make_async_copy(held, here, in_sem.at[i]) for i, (held, here) in enumerate(pairs)
    ]
    for copy in inputs:
        copy.start()
    barrier = pltpu.get_barrier_semaphore()

    def greet(k, carry):
        pl.semaphore_signal(
            barrier, inc=1, device_id=(grp, lax.rem(sub + k, n_sub)), device_id_type=MESH
        )
        return carry

    lax.fori_loop(1, n_sub, greet, 0)

    @pl.when(has_lower)
    def _():
        pl.semaphore_signal(barrier, inc=1, device_id=(grp - 1, sub), device_id_type=MESH)

    @pl.when(has_upper)
    def _():
        pl.semaphore_signal(barrier, inc=1, device_id=(grp + 1, sub), device_id_type=MESH)

    part_rows = BLK // PARTS
    loads = [
        pltpu.make_async_copy(
            a_hbm.at[pl.ds(i * part_rows, part_rows)],
            a_v.at[pl.ds(i * part_rows, part_rows)],
            a_sem.at[i],
        )
        for i in range(PARTS)
    ]
    for load in loads:
        load.start()

    inputs[0].wait()

    for c in range(CHUNKS):
        zs[c * NV:(c + 1) * NV, :] = z_ref[:, c * LANES:(c + 1) * LANES]
    source = lax.broadcasted_iota(jnp.int32, (LANES, LANES), 0)
    target = lax.broadcasted_iota(jnp.int32, (LANES, LANES), 1)
    for half in range(2):
        pick = (source == half * BS + lax.rem(target, BS)).astype(F32).astype(BF16)
        moved = jnp.dot(zs[...], pick, preferred_element_type=F32).astype(BF16)
        xn[:, half] = moved.reshape(CHUNKS, NV, LANES)
    inputs[1].wait()
    for r in range(4):
        for c in range(SEND):
            node = send_s[0, r, c]
            out_b[r, c] = xn[lax.shift_right_logical(node, 1), lax.bitwise_and(node, 1)]

    pl.semaphore_wait(
        barrier, n_sub - 1 + has_lower.astype(jnp.int32) + has_upper.astype(jnp.int32)
    )

    def ghost_copy(r, device):
        return pltpu.make_async_remote_copy(
            src_ref=out_b.at[r], dst_ref=ghost.at[r], send_sem=ghost_send.at[r],
            recv_sem=ghost_recv.at[r], device_id=device, device_id_type=MESH,
        )

    to_next = ghost_copy(0, (grp, following))
    to_prev = ghost_copy(1, (grp, previous))
    to_upper = ghost_copy(2, (lax.rem(grp + 1, n_grp), sub))
    to_lower = ghost_copy(3, (lax.rem(grp + n_grp - 1, n_grp), sub))
    to_next.start()
    to_prev.start()

    @pl.when(has_upper)
    def _():
        to_upper.start()

    @pl.when(has_lower)
    def _():
        to_lower.start()

    @pl.when(jnp.logical_not(has_lower))
    def _():
        ghost[2] = jnp.zeros((SEND, NV, LANES), BF16)

    @pl.when(jnp.logical_not(has_upper))
    def _():
        ghost[3] = jnp.zeros((SEND, NV, LANES), BF16)

    for half in range(2):
        for parity in range(2):
            wanted = half * BS + 2 * target + parity
            pick = jnp.logical_and(source == wanted, target < BS // 2).astype(F32).astype(BF16)
            moved = jnp.dot(zs[...], pick, preferred_element_type=F32).astype(BF16)
            zl[:, half, parity * NV:(parity + 1) * NV] = moved.reshape(CHUNKS, NV, LANES)

    for copy in inputs[2:]:
        copy.wait()

    diag_sum = jnp.zeros((2 * NV, NV), F32)
    rhs_sum = jnp.zeros((NV, LANES), F32)
    for c in range(CHUNKS):
        z_c = z_ref[:, c * LANES:(c + 1) * LANES]
        z_f = z_c.astype(F32)
        diag_sum = diag_sum + dot_nt(hi_lo(z_f * diag_ref[c:c + 1, :]), z_c)
        rhs_sum = rhs_sum + z_f * res_ref[c:c + 1, :]
    rhs = jnp.sum(rhs_sum, axis=1, keepdims=True) * (1.0 / 64.0)

    low_half = lax.broadcasted_iota(jnp.int32, (NV, LANES), 1) < BS
    live = live_s[0]
    acc_own[...] = diag_sum
    acc_ghost[...] = jnp.zeros_like(acc_ghost)

    def turn_own(g, carry):
        base = pl.multiple_of(g * GROUP, GROUP)
        for m in range(BS // 2):
            slab = a_v[pl.ds(base, GROUP), m * LANES:(m + 1) * LANES].astype(F32)
            wide[pl.ds(m, GROUP, stride=PITCH), :] = slab
        own_q = []
        own_x = []
        for t in range(GROUP):
            row = rows_s[0, base + t]
            left = zl[lax.shift_right_logical(row, 1), lax.bitwise_and(row, 1)][:, :BS // 2]
            block = wide[t * PITCH:t * PITCH + BS // 2, :].astype(BF16)
            both = jnp.dot(left, block, preferred_element_type=F32)
            q = jnp.where(low_half, both[:NV], both[NV:])
            q = q * (base + t < live).astype(F32)
            q = hi_lo(q)
            if t % 2 == 0:
                col = cols_s[0, base + t]
                own_q.append(q)
                own_x.append(xn[lax.shift_right_logical(col, 1), lax.bitwise_and(col, 1)])
            else:
                qs[g, t // 2] = q
        acc_own[...] += dot_nt(
            jnp.concatenate(own_q, axis=1), jnp.concatenate(own_x, axis=1)
        )
        return carry

    for load in loads:
        load.wait()
    lax.fori_loop(0, TURNS, turn_own, 0)

    to_next.wait()
    to_prev.wait()

    @pl.when(has_upper)
    def _():
        to_upper.wait_send()

    @pl.when(has_lower)
    def _():
        to_upper.wait_recv()

    @pl.when(has_lower)
    def _():
        to_lower.wait_send()

    @pl.when(has_upper)
    def _():
        to_lower.wait_recv()

    def turn_ghost(h, carry):
        for r in range(4):
            q_list = []
            x_list = []
            for e in range(2):
                g = 2 * h + e
                for t in (2 * r + 1, 2 * r + 9):
                    col = lax.bitwise_and(cols_s[0, g * GROUP + t], SEND - 1)
                    q_list.append(qs[g, t // 2])
                    x_list.append(ghost[r, col])
            acc_ghost[r] += dot_nt(
                jnp.concatenate(q_list, axis=1), jnp.concatenate(x_list, axis=1)
            )
        return carry

    lax.fori_loop(0, TURNS // 2, turn_ghost, 0)

    scale = 1.0 / ROWS
    coarse = [(acc_own[:NV] + acc_own[NV:]) * scale]
    for r in range(4):
        coarse.append((acc_ghost[r, :NV] + acc_ghost[r, NV:]) * scale)
    own, before, after = coarse[:3]
    strip[...] = jnp.concatenate(
        [
            (own + jnp.transpose(own)) * 0.5,
            before * 0.5,
            after * 0.5,
            jnp.broadcast_to(rhs, (NV, NV)),
        ],
        axis=1,
    )

    def strip_copy(k, owner):
        return pltpu.make_async_remote_copy(
            src_ref=strip, dst_ref=strips.at[owner], send_sem=strip_send.at[k],
            recv_sem=strip_recv.at[owner], device_id=(grp, lax.rem(sub + k, n_sub)),
            device_id_type=MESH,
        )

    def send(k, carry):
        strip_copy(k, sub).start()
        return carry

    lax.fori_loop(1, n_sub, send, 0)
    strips[sub] = strip[...]
    for o in range(5):
        blocks[o * NV:(o + 1) * NV, :] = jnp.concatenate([coarse[o]] * 4, axis=1)

    def finish(k, carry):
        strip_copy(k, sub).wait_send()
        strip_copy(k, lax.rem(sub + n_sub - k, n_sub)).wait_recv()
        return carry

    lax.fori_loop(1, n_sub, finish, 0)


def eliminate(work):
    row_of = lax.broadcasted_iota(jnp.int32, (1, NV, LANES), 1)
    for k in range(0, NV, PIVOTS):
        span = range(PIVOTS)
        cols = [jnp.broadcast_to(work[:, :, k + j:k + j + 1], work.shape) for j in span]
        small = [[cols[j][:, k + i:k + i + 1, :] for j in span] for i in span]
        rows = [work[:, k + i:k + i + 1, :] for i in span]
        for i in span:
            inverse = 1.0 / small[i][i]
            rows[i] = rows[i] * inverse
            for j in range(i + 1, PIVOTS):
                small[i][j] = small[i][j] * inverse
            for l in span:
                if l != i:
                    rows[l] = rows[l] - small[l][i] * rows[i]
                    for j in range(i + 1, PIVOTS):
                        small[l][j] = small[l][j] - small[l][i] * small[i][j]
        rest = work
        for j in span:
            rest = rest - cols[j] * rows[j]
        for i in span:
            rest = jnp.where(row_of == k + i, rows[i], rest)
        work = rest
    return work


def dot_exact(a, b):
    return jnp.dot(a, b, precision=HIGHEST_PREC, preferred_element_type=F32)


def solve_blocks(systems):
    count = len(systems)
    if count == 1:
        return [eliminate(systems[0][None])[0][:, 3 * NV:]]
    odd = eliminate(jnp.stack(systems[1::2]))
    half = count // 2
    reduced = []
    zero = jnp.zeros((NV, NV), F32)
    for i in range(half):
        even = systems[2 * i]
        ahead, behind = odd[i], odd[(i - 1) % half]
        to_next, to_prev = even[:, 2 * NV:3 * NV], even[:, NV:2 * NV]
        if count == 2:
            gone = dot_exact(to_next + to_prev, ahead)
            link = gone[:, NV:2 * NV] + gone[:, 2 * NV:3 * NV]
            reduced.append(even - jnp.concatenate([link, zero, zero, gone[:, 3 * NV:]], axis=1))
            continue
        up = dot_exact(to_next, ahead)
        down = dot_exact(to_prev, behind)
        diag = even[:, :NV] - up[:, NV:2 * NV] - down[:, 2 * NV:3 * NV]
        right = even[:, 3 * NV:] - up[:, 3 * NV:] - down[:, 3 * NV:]
        reduced.append(
            jnp.concatenate([diag, -down[:, NV:2 * NV], -up[:, 2 * NV:3 * NV], right], axis=1)
        )
    evens = solve_blocks(reduced)
    solved = []
    for i in range(half):
        left, right = evens[i], evens[(i + 1) % half]
        gone = dot_exact(odd[i][:, NV:2 * NV], left) + dot_exact(odd[i][:, 2 * NV:3 * NV], right)
        solved += [left, odd[i][:, 3 * NV:] - gone]
    return solved


def solve_kernel(n_sub, strips, blocks, z_ref, corr, rows_out, found):
    systems = []
    zero = jnp.zeros((NV, NV), F32)
    flipped = [jnp.transpose(strips[s]) for s in range(n_sub)]
    for s in range(n_sub):
        from_prev = flipped[(s - 1) % n_sub][2 * NV:3 * NV]
        from_next = flipped[(s + 1) % n_sub][NV:2 * NV]
        systems.append(strips[s] + jnp.concatenate([zero, from_prev, from_next, zero], axis=1))
    solved = solve_blocks(systems)
    for s in range(n_sub):
        found[s] = jnp.concatenate([solved[s]] * 4, axis=1)
    own = found[lax.axis_index("sub")]
    for c in range(CHUNKS):
        z_c = z_ref[:, c * LANES:(c + 1) * LANES].astype(F32)
        corr[c:c + 1, :] = jnp.sum(z_c * own, axis=0, keepdims=True)
    lane8 = lax.broadcasted_iota(jnp.int32, (8, LANES), 1)
    for o in range(5):
        total = blocks[pl.ds(o * NV, 8, stride=4), :]
        for q in range(1, 4):
            total = jnp.where(
                lane8 >= q * NV, blocks[pl.ds(o * NV + q, 8, stride=4), :], total
            )
        rows_out[o * 8:(o + 1) * 8, :] = total


def per_device(
    n_grp, n_sub, deflation, operator_blocks, diagonal, block_rows, block_cols, live_count,
    send_blocks, residual,
):
    vmem = pl.BlockSpec(memory_space=pltpu.VMEM)
    strips, blocks = pl.pallas_call(
        functools.partial(assemble_kernel, n_grp, n_sub),
        out_shape=(
            jax.ShapeDtypeStruct((n_sub, NV, LANES), F32),
            jax.ShapeDtypeStruct((5 * NV, LANES), F32),
        ),
        in_specs=[pl.BlockSpec(memory_space=pltpu.SMEM)]
        + [pl.BlockSpec(memory_space=pltpu.HBM)] * 7,
        out_specs=(vmem, vmem),
        scratch_shapes=[
            pltpu.SMEM((1, BLK), jnp.int32),
            pltpu.SMEM((1, BLK), jnp.int32),
            pltpu.SMEM((1, 4, SEND), jnp.int32),
            pltpu.VMEM((NV, ROWS), BF16),
            pltpu.VMEM((CHUNKS, LANES), F32),
            pltpu.VMEM((CHUNKS, LANES), F32),
            pltpu.SemaphoreType.DMA((6,)),
            pltpu.VMEM((BLK, BS * BS), BF16),
            pltpu.VMEM((CHUNKS * NV, LANES), BF16),
            pltpu.VMEM((CHUNKS, 2, 2 * NV, LANES), BF16),
            pltpu.VMEM((CHUNKS, 2, NV, LANES), BF16),
            pltpu.VMEM((4, SEND, NV, LANES), BF16),
            pltpu.VMEM((4, SEND, NV, LANES), BF16),
            pltpu.VMEM((GROUP * PITCH, LANES), F32),
            pltpu.VMEM((TURNS, GROUP // 2, 2 * NV, LANES), BF16),
            pltpu.VMEM((NV, LANES), F32),
            pltpu.VMEM((2 * NV, NV), F32),
            pltpu.VMEM((4, 2 * NV, NV), F32),
            pltpu.SemaphoreType.DMA((PARTS,)),
            pltpu.SemaphoreType.DMA((4,)),
            pltpu.SemaphoreType.DMA((4,)),
            pltpu.SemaphoreType.DMA((n_sub,)),
            pltpu.SemaphoreType.DMA((n_sub,)),
        ],
        compiler_params=pltpu.CompilerParams(
            collective_id=0, has_side_effects=True, vmem_limit_bytes=40 * 2**20
        ),
    )(
        live_count,
        *[
            pltpu.with_memory_space_constraint(held, pltpu.HBM)
            for held in (
                block_rows, block_cols, send_blocks, deflation,
                diagonal.reshape(CHUNKS, LANES), residual.reshape(CHUNKS, LANES), operator_blocks,
            )
        ],
    )
    correction, coarse_rows = pl.pallas_call(
        functools.partial(solve_kernel, n_sub),
        out_shape=(
            jax.ShapeDtypeStruct((CHUNKS, LANES), F32),
            jax.ShapeDtypeStruct((5 * NV * NV // LANES, LANES), F32),
        ),
        in_specs=[vmem] * 3,
        out_specs=(vmem, vmem),
        scratch_shapes=[pltpu.VMEM((n_sub, NV, LANES), F32)],
        compiler_params=pltpu.CompilerParams(vmem_limit_bytes=40 * 2**20),
    )(strips, blocks, deflation)
    return correction.reshape(ROWS), coarse_rows.reshape(1, 5 * NV * NV)


def solution(mesh):
    placed = (
        P(None, ("grp", "sub")),
        P(("grp", "sub"), None),
        P(("grp", "sub")),
        P(("grp", "sub"), None),
        P(("grp", "sub"), None),
        P(("grp", "sub")),
        P(("grp", "sub"), None, None),
        P(("grp", "sub")),
    )
    return jax.shard_map(
        functools.partial(per_device, mesh.shape["grp"], mesh.shape["sub"]),
        mesh=mesh,
        in_specs=placed,
        out_specs=(P(("grp", "sub")), P(("grp", "sub"), None)),
        check_vma=False,
    )
```
